512 devices in a mesh: rep: 16 (over y, x_lo), shard: 32 (over x_hi, z, core).
Axes of the slice: x: 4 (x_hi: 2, x_lo: 2; x = x_hi * 2 + x_lo), y: 8, z: 8, core: 2. Of those that a mesh axis runs over, the one named last changes fastest.
Arguments:
- pooled_cot: bfloat16 [32768, 32, 256], P(('rep', 'shard')), may hold values from -6 to 6
- bag_ids: int32 [32768, 32, 2], P('rep', 'shard'), may hold values from 0 to 3071, as said below
- table: bfloat16 [98304, 256], P('shard'), may hold values from -3 to 3
- accum: float32 [98304], P('shard'), may hold values from 0.5 to 8
- listed_block_index: int32 [16, 64], P('rep', 'shard'), may hold values from 0 to 23, as said below
- counts: int32 [16, 32], P('rep', 'shard'), may hold values from 1 to 2, as said below
- x_zero: bfloat16 [32768, 256], P(('rep', 'shard')), may hold values from -6 to 6
- w_top: bfloat16 [256, 2048], replicated, may hold values from -0.375 to 0.375
- u_proj: bfloat16 [256, 256], replicated, may hold values from -0.375 to 0.375
- v_proj: bfloat16 [256, 256], replicated, may hold values from -0.375 to 0.375
- cross_bias: float32 [256], replicated, may hold values from -3 to 3
- d_act: bfloat16 [32768, 2048], P(('rep', 'shard')), may hold values from -24 to 24
Outputs:
- new_table: bfloat16 [98304, 256], P('shard')
- new_accum: float32 [98304], P('shard')
- dense_grad: float32 [655360], P(('rep', 'shard'))
The draws below stay inside these ranges and needn't reach their ends.
Inputs may be any that keep to these rules, and one draw needn't show every extreme that they name: `listed_block_index`: each device's first counts slots name distinct blocks of its slab, the remaining slots repeat arbitrary blocks. `counts`: live slots of each device; in every replica some device has all 2 live. `bag_ids`: every id lies in a block of a live slot of the device that owns its feature in its sample's replica.
All inputs are finite; a program needn't handle non-finite values.
Results may differ from the reference program's by a relative error of at most 0.0071.
Values may be sent and summed in bfloat16 or wider, within the bound.
A program may use at most 64 MiB of HBM per device.

```python
import math
import jax
import jax.numpy as jnp
from jax import lax

E = 256
DX = 256
HID = 2048
RANK = 256
B_DEV = 64
ROWS_DEV = 3072
FEAT_DEV = 1
H = 2
BLOCK_ROWS = 128
NB_PAD = 2
NBLK = 24
F = 32
SAMPLES = 32768
N_REP = 16
N_SHARD = 32


def slot_tables(key):
    count_key = jax.random.fold_in(key, 11)
    order_key = jax.random.fold_in(key, 12)
    filler_key = jax.random.fold_in(key, 13)
    active_flags = jax.random.randint(count_key, (N_REP, N_SHARD), 1, NB_PAD + 1)
    active_flags = active_flags.at[:, 0].set(NB_PAD).astype(jnp.int32)
    scores = jax.random.randint(order_key, (N_REP, N_SHARD, NBLK), 0, 1048576) * NBLK + jnp.arange(NBLK)[None, None, :]
    order = jnp.argsort(scores, axis=-1, stable=True).astype(jnp.int32)
    filler = jax.random.randint(filler_key, (N_REP, N_SHARD, NB_PAD), 0, NBLK).astype(jnp.int32)
    slots = jnp.arange(NB_PAD)[None, None, :]
    listed = jnp.where(slots < active_flags[:, :, None], order[:, :, :NB_PAD], filler)
    return (active_flags, order, listed)


def draw_counts(key, part):
    active_flags, order, listed = slot_tables(key)
    return active_flags


def draw_listed_block_index(key, part):
    active_flags, order, listed = slot_tables(key)
    return listed.reshape(N_REP, N_SHARD * NB_PAD)


def draw_bag_ids(key, part):
    active_flags, order, listed = slot_tables(key)
    key = jax.random.fold_in(key, 5)
    first_key, second_key, row_key = jax.random.split(key, 3)
    replica = jnp.arange(SAMPLES) // (N_SHARD * B_DEV)
    owner = jnp.arange(F) // FEAT_DEV
    live_here = active_flags[replica[:, None], owner[None, :]]
    first = jax.random.randint(first_key, (SAMPLES, F, H), 0, 720720) % live_here[:, :, None]
    second = jax.random.randint(second_key, (SAMPLES, F, H), 0, 720720) % live_here[:, :, None]
    slot = jnp.minimum(first, second)
    block = order[replica[:, None, None], owner[None, :, None], slot]
    offset = jax.random.randint(row_key, (SAMPLES, F, H), 0, BLOCK_ROWS)
    return (block * BLOCK_ROWS + offset).astype(jnp.int32)


def strengthened(drawn, rng, source, target, shards_of, factor):
    owner, partner = [(jnp.arange(drawn.shape[axis_at]) // (drawn.shape[axis_at] // shards_of)).reshape([-1 if axis == axis_at else 1 for axis in range(drawn.ndim)]) for axis_at in (source, target)]
    chosen = jax.random.permutation(rng, shards_of)[partner]
    strong = (owner == chosen) | (owner == (partner + shards_of // 2) % shards_of)
    return jnp.where(strong, factor * drawn, drawn)


def steps_of(stream_key, extent, cuts, low, largest):
    def one(dim, blocks):
        heights = jax.random.uniform(jax.random.fold_in(jax.random.fold_in(stream_key, 6), dim), (blocks,), jnp.float32, low / len(cuts), largest / len(cuts))
        return jnp.repeat(jnp.exp(heights), extent[dim] // blocks).reshape((-1,) + (1,) * (len(extent) - dim - 1))

    gain = one(*cuts[0])
    for cut in cuts[1:]:
        gain = gain * one(*cut)
    return gain


def bell_draw(rng, shape, width, most, cuts=(), held_as=jnp.bfloat16):
    entries = jax.random.normal(rng, shape, jnp.float32) * width
    if len(cuts) > 0:
        entries = steps_of(rng, shape, cuts, -0.22, 0.18) * entries
    return jnp.clip(entries, min=-most, max=most).astype(held_as)


def gaussian_with(key, dims, deviation, bound, cuts, heavy, held_as=jnp.bfloat16):
    result = deviation * jax.random.normal(key, dims, jnp.float32)
    if cuts:
        result = result * steps_of(key, dims, cuts, -0.22, 0.18)
    return jnp.clip(strengthened(result, jax.random.fold_in(key, 3), *heavy), -bound, bound).astype(held_as)


def setup_inputs(seed: int = 0) -> dict:
    streams_of = jax.random.split(jax.random.key(seed), 13)
    return {
        "pooled_cot": bell_draw(streams_of[0], (SAMPLES, F, E), 1.0, 6.0, ((0, 512),)),
        "bag_ids": draw_bag_ids(jax.random.fold_in(streams_of[12], 71), 0),
        "table": bell_draw(streams_of[2], (N_SHARD * ROWS_DEV, E), 0.5, 3.0, ((0, 32),)),
        "accum": jnp.clip(jnp.exp(math.log(8.0) - 2.7725887 * jax.random.uniform(streams_of[3], (N_SHARD * ROWS_DEV,), jnp.float32) ** steps_of(streams_of[3], (N_SHARD * ROWS_DEV,), ((0, 32),), -0.2, 0.2)), 0.5, 8.0),
        "listed_block_index": draw_listed_block_index(jax.random.fold_in(streams_of[12], 71), 0),
        "counts": draw_counts(jax.random.fold_in(streams_of[12], 71), 0),
        "x_zero": bell_draw(streams_of[6], (SAMPLES, DX), 1.0, 6.0, ((0, 512),)),
        "w_top": bell_draw(streams_of[7], (DX, HID), DX ** -0.5, 0.375),
        "u_proj": bell_draw(streams_of[8], (DX, RANK), RANK ** -0.5, 0.375),
        "v_proj": bell_draw(streams_of[9], (DX, RANK), DX ** -0.5, 0.375),
        "cross_bias": bell_draw(streams_of[10], (DX,), 0.5, 3.0, (), jnp.float32),
        "d_act": gaussian_with(streams_of[11], (SAMPLES, HID), 1.0, 24.0, ((0, 512),), (0, 1, 512, 6.0)),
    }


learn_rate = 0.5

def widen(a):
    return a.astype(jnp.float32)

def rounded(a):
    return lax.optimization_barrier(a.astype(jnp.bfloat16)).astype(jnp.float32)

def dense_terms(x_zero, w_top, u_proj, v_proj, cross_bias, d_act):
    high = lax.Precision.HIGHEST
    x_in = widen(x_zero)
    hid = rounded(jnp.dot(x_in, widen(v_proj), precision=high))
    mixed = jnp.dot(hid, widen(u_proj).T, precision=high) + cross_bias
    x_one = rounded(x_in * mixed + x_in)
    z_pre = jnp.dot(x_one, widen(w_top), precision=high)
    sigma = jax.nn.sigmoid(z_pre)
    d_pre = rounded(widen(d_act) * sigma * (1.0 + z_pre * (1.0 - sigma)))
    grad_w = jnp.dot(d_pre.T, x_one, precision=high)
    back_x = jnp.dot(d_pre, widen(w_top).T, precision=high)
    d_mix = rounded(back_x * x_in)
    grad_u = jnp.dot(d_mix.T, hid, precision=high)
    d_hid = rounded(jnp.dot(d_mix, widen(u_proj), precision=high))
    grad_v = jnp.dot(x_in.T, d_hid, precision=high)
    return jnp.concatenate([grad_w.ravel(), grad_u.ravel(), grad_v.ravel()])

def reference(pooled_cot, bag_ids, table, accum, listed_block_index, counts, x_zero, w_top, u_proj, v_proj, cross_bias, d_act):
    group = N_SHARD * B_DEV
    owner = (jnp.arange(F) // FEAT_DEV).astype(jnp.int32)
    table_f = widen(table)
    pooled_g = pooled_cot.reshape(N_REP, group, F, E)
    ids_g = bag_ids.reshape(N_REP, group, F, H)
    lists = listed_block_index.reshape(N_REP, N_SHARD, NB_PAD)

    def replica(carry, pieces):
        pooled_r, ids_r, list_r, count_r = pieces
        active_flags = jnp.arange(NB_PAD)[None, :] < count_r[:, None]
        match = (list_r[:, :, None] == jnp.arange(NBLK)[None, None, :]) & active_flags[:, :, None]
        block_live = jnp.any(match, axis=1)
        grad = jnp.zeros((N_SHARD * ROWS_DEV, E), jnp.float32)
        for pos in range(H):
            ids_h = ids_r[:, :, pos]
            keep = block_live[owner[None, :], ids_h // BLOCK_ROWS]
            values = widen(pooled_r) * keep[:, :, None].astype(jnp.float32)
            target = owner[None, :] * ROWS_DEV + ids_h
            grad = grad + jax.ops.segment_sum(values.reshape(group * F, E), target.reshape(group * F), num_segments=N_SHARD * ROWS_DEV)
        acc_r = accum + lax.optimization_barrier(jnp.mean(grad * grad, axis=1))
        row_r = (table_f - learn_rate * grad * lax.rsqrt(acc_r)[:, None]).astype(jnp.bfloat16)
        return ((carry[0] + (widen(row_r) - table_f), carry[1] + (acc_r - accum)), None)
    start = (jnp.zeros((N_SHARD * ROWS_DEV, E), jnp.float32), jnp.zeros((N_SHARD * ROWS_DEV,), jnp.float32))
    sums, _ = lax.scan(replica, start, (pooled_g, ids_g, lists, counts))
    new_table = (table_f + sums[0] / N_REP).astype(jnp.bfloat16)
    new_accum = accum + sums[1] / N_REP

    def dense_part(pieces):
        return dense_terms(pieces[0], w_top, u_proj, v_proj, cross_bias, pieces[1])
    terms = lax.map(dense_part, (x_zero.reshape(N_REP, group, DX), d_act.reshape(N_REP, group, HID)))
    dense_grad = lax.optimization_barrier(jnp.sum(terms, axis=0)) * (1.0 / jnp.sqrt(jnp.float32(SAMPLES)))
    return (new_table, new_accum, dense_grad)
```

```python
import functools

import jax
import jax.numpy as jnp
from jax import lax
from jax.experimental import pallas as pl
from jax.experimental.pallas import tpu as pltpu
from jax.sharding import PartitionSpec as P

MESH = pl.DeviceIdType.MESH
BLOCK = 128
NS = 32
NR = 16
NY = 8
LEARN = 0.5
BF = jnp.bfloat16
F32 = jnp.float32


def remote(src, dst, send, recv, rep, shard):
    return pltpu.make_async_remote_copy(
        src_ref=src,
        dst_ref=dst,
        send_sem=send,
        recv_sem=recv,
        device_id={"rep": rep, "shard": shard},
        device_id_type=MESH,
    )


def matmul(a, b):
    return jnp.dot(a, b, preferred_element_type=F32)


def matmul_nt(a, b):
    return lax.dot_general(a, b, (((1,), (1,)), ((), ())), preferred_element_type=F32)


def matmul_tn(a, b):
    return lax.dot_general(a, b, (((0,), (0,)), ((), ())), preferred_element_type=F32)


def exchange(
    pooled,
    ids,
    accum,
    listed,
    counts,
    xz,
    w_top,
    u_proj,
    v_proj,
    bias,
    d_act,
    rows_out,
    stats_out,
    blocks_out,
    dense_out,
    wide,
    a_src,
    a_dst,
    hits,
    cols,
    l_dst,
    x_dst,
    part,
    part_dst,
    a_send,
    a_recv,
    l_send,
    l_recv,
    x_send,
    x_recv,
    own_sem,
    c_send,
    c_recv,
    st_send,
    st_recv,
    p_send,
    p_recv,
):
    rep = lax.axis_index("rep")
    shard = lax.axis_index("shard")

    barrier = pltpu.get_barrier_semaphore()

    @pl.loop(1, NS)
    def _(p):
        pl.semaphore_signal(
            barrier, inc=1, device_id={"rep": rep, "shard": lax.rem(shard + p, NS)}, device_id_type=MESH
        )

    @pl.loop(1, NR)
    def _(p):
        pl.semaphore_signal(
            barrier, inc=1, device_id={"rep": lax.rem(rep + p, NR), "shard": shard}, device_id_type=MESH
        )

    samples, feats, width = pooled.shape
    for c in range(0, samples, 16):
        taken = pooled[c : c + 16].astype(F32).reshape(16 * feats, width)
        wide[0, pl.ds(c * feats, 16 * feats), :] = taken[:, :128]
        wide[1, pl.ds(c * feats, 16 * feats), :] = taken[:, 128:]

    pl.semaphore_wait(barrier, NS + NR - 2)

    def pick(h, f):
        return wide[h, pl.ds(f, samples, stride=feats), :].astype(BF)

    def a_out(h, p):
        t = lax.rem(shard + p, NS)
        return remote(a_src.at[h, t], a_dst.at[h, shard], a_send.at[h, p], a_recv.at[h, shard], rep, t)

    def a_in(h, p):
        t = lax.rem(shard + p, NS)
        return remote(a_src.at[h, t], a_dst.at[h, t], a_send.at[h, p], a_recv.at[h, t], rep, t)

    @pl.loop(1, NS)
    def _(p):
        t = lax.rem(shard + p, NS)
        a_src[0, t] = pick(0, t)
        a_out(0, p).start()

    @pl.loop(1, NS)
    def _(p):
        t = lax.rem(shard + p, NS)
        a_src[1, t] = pick(1, t)
        a_out(1, p).start()

    for h in range(2):
        a_dst[h, shard] = pick(h, shard)

    def x_copy(p, slot):
        t = lax.rem(rep + p, NR)
        return remote(xz, x_dst.at[slot(t)], x_send.at[p], x_recv.at[slot(t)], t, shard)

    def l_copy(p, slot):
        t = lax.rem(rep + p, NR)
        at = pl.multiple_of(((5 * t) // 4) * 128, 128)
        return remote(cols.at[:, pl.ds(at, 256)], l_dst.at[slot(t)], l_send.at[p], l_recv.at[slot(t)], t, shard)

    mine, theirs = (lambda t: rep), (lambda t: t)

    @pl.loop(1, NR)
    def _(p):
        x_copy(p, mine).start()

    x = xz[...]
    x_dst[rep] = x
    x_wide = x.astype(F32)
    hid = matmul(x, v_proj[...]).astype(BF)
    mixed = matmul_nt(hid, u_proj[...]) + bias[...]
    x_one = (x_wide * mixed + x_wide).astype(BF)
    hidden = d_act.shape[1]
    back = jnp.zeros((samples, width), F32)
    for c in range(0, hidden, 512):
        z = matmul(x_one, w_top[:, c : c + 512])
        sig = jax.nn.sigmoid(z)
        dz = (d_act[:, c : c + 512].astype(F32) * sig * (1.0 + z * (1.0 - sig))).astype(BF)
        cols[:, c : c + 512] = dz
        back = back + matmul_nt(dz, w_top[:, c : c + 512])
    dp = (back * x_wide).astype(BF)
    cols[:, hidden : hidden + width] = dp
    cols[:, hidden + width : hidden + 2 * width] = dp

    @pl.loop(1, NR)
    def _(p):
        l_copy(p, mine).start()

    own_at = pl.multiple_of(((5 * rep) // 4) * 128, 128)
    own_copy = pltpu.make_async_copy(cols.at[:, pl.ds(own_at, 256)], l_dst.at[rep], own_sem)
    own_copy.start()

    slots = listed.shape[1]
    lookups = ids.shape[1]
    for k in range(slots):
        first = jnp.where(counts[0, 0] > k, listed[0, k] * BLOCK, -(1 << 20))
        for c in range(0, lookups, 512):
            rel = ids[:, c : c + 512] - first
            row = lax.broadcasted_iota(jnp.int32, (BLOCK, 512), 0)
            hit = jnp.zeros((BLOCK, 512), F32)
            for pos in range(ids.shape[0]):
                hit = hit + jnp.where(row == rel[pos : pos + 1, :], 1.0, 0.0)
            hits[k * BLOCK : (k + 1) * BLOCK, c : c + 512] = hit.astype(BF)

    y = rep // 2
    xl = lax.rem(rep, 2)

    def at(dy, flip):
        return lax.rem(y + dy + NY, NY) * 2 + ((1 - xl) if flip else xl)

    up, down, across = at(1, False), at(-1, False), at(0, True)
    started = []
    counter = [0]

    def ref_of(h, q, half):
        if half is None:
            return rows_out.at[h, q]
        return rows_out.at[h, q, pl.ds(half * BLOCK, BLOCK)]

    def c_start(h, q, to, half=None):
        copy = remote(
            ref_of(h, q, half), ref_of(h, q, half), c_send.at[counter[0]], c_recv.at[h, q, half or 0], to, shard
        )
        counter[0] += 1
        copy.start()
        started.append(copy)

    def c_wait(h, q, half=None):
        remote(ref_of(h, q, half), ref_of(h, q, half), c_send.at[0], c_recv.at[h, q, half or 0], across, shard).wait_recv()

    def step1(h):
        for to in (up, down, across):
            c_start(h, rep, to)

    def step2(h):
        for dy, to in ((-1, up), (1, down)):
            c_wait(h, at(dy, False))
            c_start(h, at(dy, False), to)
        c_wait(h, across)
        for to in (up, down):
            c_start(h, across, to)

    def step3(h):
        for dy, to in ((-1, up), (1, down)):
            c_wait(h, at(2 * dy, False))
            c_start(h, at(2 * dy, False), to)
        for dy, to in ((-1, up), (1, down)):
            c_wait(h, at(dy, True))
            c_start(h, at(dy, True), to)

    def step4(h):
        for dy, to, half in ((-1, up, 0), (1, down, 1)):
            c_wait(h, at(3 * dy, False))
            c_start(h, at(3 * dy, False), to, half)
            c_start(h, at(3 * dy, False), across)

    def step5(h):
        for half in (0, 1):
            c_wait(h, at(4, False), half)
            c_start(h, at(4, False), across, half)

    def step6(h):
        for dy in (-2, 2, -3, 3):
            c_wait(h, at(dy, True))
        for half in (0, 1):
            c_wait(h, at(4, True), half)

    def gradient(h):
        @pl.loop(1, NS)
        def _(p):
            a_in(h, p).wait_recv()

        grad = matmul(hits[...], a_dst[h].reshape(lookups, 128))
        rows_out[h, rep] = grad.astype(BF)
        step1(h)
        return jnp.sum(grad * grad, axis=1, keepdims=True)

    square = gradient(0)
    step2(0)
    step3(0)
    square = (square + gradient(1)) * (1.0 / width)

    diag = lax.broadcasted_iota(jnp.int32, (BLOCK, BLOCK), 0) == lax.broadcasted_iota(jnp.int32, (BLOCK, BLOCK), 1)
    change, scale, block = [], [], []
    for k in range(slots):
        col = jnp.broadcast_to(square[k * BLOCK : (k + 1) * BLOCK], (BLOCK, BLOCK))
        mean = jnp.sum(jnp.where(diag, col, 0.0), axis=0, keepdims=True)
        old = accum[pl.ds(listed[0, k], 1), :]
        change.append(mean)
        scale.append(LEARN * lax.rsqrt(old + mean))
        block.append(jnp.full((1, BLOCK), listed[0, k].astype(F32), F32))
    stats_out[rep] = jnp.concatenate(change + scale + block + [jnp.zeros((2, BLOCK), F32)], axis=0)

    def st_copy(p, slot):
        t = lax.rem(rep + p, NR)
        return remote(stats_out.at[slot(t)], stats_out.at[slot(t)], st_send.at[p], st_recv.at[slot(t)], t, shard)

    @pl.loop(1, NR)
    def _(p):
        st_copy(p, mine).start()

    step4(0)
    step2(1)
    step5(0)
    step3(1)
    step4(1)

    @pl.loop(1, NR)
    def _(p):
        x_copy(p, theirs).wait_recv()
        l_copy(p, theirs).wait_recv()

    own_copy.wait()
    many = NR * samples
    xs = x_dst[...].reshape(many, width)
    ls = l_dst[...].reshape(many, width)
    xs_wide = xs.astype(F32)
    hids = matmul(xs, v_proj[...]).astype(BF)
    ones = (xs_wide * (matmul_nt(hids, u_proj[...]) + bias[...]) + xs_wide).astype(BF)
    low, high = u_proj[: width // 2, :], u_proj[width // 2 :, :]
    swapped = rep == 14
    dhs = (
        matmul(ls[:, : width // 2], jnp.where(swapped, high, low))
        + matmul(ls[:, width // 2 :], jnp.where(swapped, low, high))
    ).astype(BF)
    source = lax.broadcasted_iota(jnp.int32, (width, width), 0)
    target = lax.broadcasted_iota(jnp.int32, (width, width), 1)
    wanted = (target // 8) * 5 + target % 8

    def spread(values, offset):
        chosen = (source == wanted + offset) & (target % 8 < 5)
        return matmul(values, jnp.where(chosen, 1.0, 0.0).astype(BF)).astype(BF)

    left_a = spread(ls, 32 * lax.rem(rep, 4))
    total_a = matmul_tn(left_a, jnp.where(rep <= 12, ones, hids))
    offset_b = jnp.where(rep == 12, 0, jnp.where(rep == 14, -64, 96))
    left_b = spread(jnp.where(rep <= 12, ls, xs), offset_b)
    total_b = matmul_tn(left_b, jnp.where(rep <= 12, hids, dhs))
    limit = jnp.where(rep == 12, 128, jnp.where(rep == 14, 64, jnp.where(rep == 15, 0, 160)))
    line = lax.broadcasted_iota(jnp.int32, (width, width), 0)
    grow = jnp.where((line // 8) * 5 + line % 8 < limit, total_a, total_b)
    part[...] = grow.reshape(NS, 8, width)
    part_dst[shard] = part[shard]

    def p_copy(p, slot):
        t = lax.rem(shard + p, NS)
        return remote(part.at[t], part_dst.at[slot(t)], p_send.at[p], p_recv.at[slot(t)], rep, t)

    own_shard, that_shard = (lambda t: shard), (lambda t: t)

    @pl.loop(1, NS)
    def _(p):
        p_copy(p, own_shard).start()

    step5(1)
    step6(0)
    step6(1)

    @pl.loop(1, NR)
    def _(p):
        st_copy(p, theirs).wait_recv()

    lane = lax.broadcasted_iota(jnp.int32, (1, BLOCK), 1)
    blocks = jnp.zeros((1, BLOCK), F32)
    for r in range(NR):
        for k in range(slots):
            row = stats_out[r, 2 * slots + k : 2 * slots + k + 1, :]
            blocks = blocks + jnp.where(lane == r * slots + k, row, 0.0)
    blocks_out[...] = blocks.astype(jnp.int32)

    @pl.loop(1, NS)
    def _(p):
        p_copy(p, that_shard).wait_recv()

    dense_out[...] = jnp.sum(part_dst[...], axis=0)

    @pl.loop(1, NS)
    def _(p):
        a_out(0, p).wait_send()
        a_out(1, p).wait_send()
        p_copy(p, own_shard).wait_send()

    @pl.loop(1, NR)
    def _(p):
        x_copy(p, mine).wait_send()
        l_copy(p, mine).wait_send()
        st_copy(p, mine).wait_send()

    for copy in started:
        copy.wait_send()


def apply(norm, blocks, table, accum, rows, stats, dense, table_out, accum_out, dense_out, total, state):
    nblk, block, width = table.shape
    reps = rows.shape[1]
    slots = 2
    total[...] = jnp.zeros_like(total)
    state[...] = jnp.zeros_like(state)
    for r in range(reps):
        scales = jnp.transpose(jnp.concatenate([stats[r, :, :]] * 16, axis=0))
        for k in range(slots):
            b = blocks[0, r * slots + k]
            col = scales[:, slots + k : slots + k + 1]
            for h in range(2):
                g = rows[h, r, k * block : (k + 1) * block, :].astype(F32)
                total[b, :, h * 128 : (h + 1) * 128] += g * col
            state[pl.ds(b, 1), :] += stats[r, k : k + 1, :]
    for b in range(nblk):
        table_out[b] = (table[b].astype(F32) - total[b] * (1.0 / reps)).astype(BF)
    accum_out[...] = accum[...] + state[...] * (1.0 / reps)
    for j in range(5):
        for h in range(2):
            dense_out[2 * j + h : 2 * j + h + 1, :] = dense[j : j + 1, h * 128 : (h + 1) * 128] * norm


def on_device(
    pooled_cot,
    bag_ids,
    table,
    accum,
    listed_block_index,
    counts,
    x_zero,
    w_top,
    u_proj,
    v_proj,
    cross_bias,
    d_act,
):
    width = table.shape[1]
    nblk = table.shape[0] // BLOCK
    samples, feats = pooled_cot.shape[:2]
    hidden = d_act.shape[1]
    slots = listed_block_index.shape[1]
    listed_rows = slots * BLOCK
    lookups = bag_ids.shape[0]
    vmem = pl.BlockSpec(memory_space=pltpu.VMEM)
    smem = pl.BlockSpec(memory_space=pltpu.SMEM)
    dma = pltpu.SemaphoreType.DMA
    ids = jnp.transpose(bag_ids.reshape(lookups, bag_ids.shape[2]))
    state = accum.reshape(nblk, BLOCK)
    rows, stats, blocks, dense = pl.pallas_call(
        exchange,
        out_shape=(
            jax.ShapeDtypeStruct((2, NR, listed_rows, 128), BF),
            jax.ShapeDtypeStruct((NR, 8, BLOCK), F32),
            jax.ShapeDtypeStruct((1, BLOCK), jnp.int32),
            jax.ShapeDtypeStruct((8, width), F32),
        ),
        in_specs=[vmem, vmem, vmem, smem, smem, vmem, vmem, vmem, vmem, vmem, vmem],
        out_specs=(vmem, vmem, vmem, vmem),
        scratch_shapes=[
            pltpu.VMEM((2, samples * feats, 128), F32),
            pltpu.VMEM((2, NS, samples, 128), BF),
            pltpu.VMEM((2, NS, samples, 128), BF),
            pltpu.VMEM((listed_rows, lookups), BF),
            pltpu.VMEM((samples, hidden + 2 * width), BF),
            pltpu.VMEM((NR, samples, width), BF),
            pltpu.VMEM((NR, samples, width), BF),
            pltpu.VMEM((NS, 8, width), F32),
            pltpu.VMEM((NS, 8, width), F32),
            dma((2, NS)),
            dma((2, NS)),
            dma((NR,)),
            dma((NR,)),
            dma((NR,)),
            dma((NR,)),
            dma,
            dma((64,)),
            dma((2, NR, 2)),
            dma((NR,)),
            dma((NR,)),
            dma((NS,)),
            dma((NS,)),
        ],
        compiler_params=pltpu.CompilerParams(
            collective_id=0, has_side_effects=True, vmem_limit_bytes=40 << 20
        ),
        name="exchange",
    )(
        pooled_cot,
        ids,
        state,
        listed_block_index,
        counts,
        x_zero,
        w_top,
        u_proj,
        v_proj,
        cross_bias.reshape(1, width),
        d_act,
    )
    total = samples * lax.axis_size("rep") * lax.axis_size("shard")
    new_table, new_accum, out = pl.pallas_call(
        functools.partial(apply, float(total) ** -0.5),
        out_shape=(
            jax.ShapeDtypeStruct((nblk, BLOCK, width), BF),
            jax.ShapeDtypeStruct((nblk, BLOCK), F32),
            jax.ShapeDtypeStruct((10, 128), F32),
        ),
        in_specs=[smem, vmem, vmem, vmem, vmem, vmem],
        out_specs=(vmem, vmem, vmem),
        scratch_shapes=[pltpu.VMEM((nblk, BLOCK, width), F32), pltpu.VMEM((nblk, BLOCK), F32)],
        compiler_params=pltpu.CompilerParams(vmem_limit_bytes=24 << 20),
        name="apply",
    )(blocks, table.reshape(nblk, BLOCK, width), state, rows, stats, dense)
    return (new_table.reshape(table.shape), new_accum.reshape(accum.shape), out.reshape(1280))


def solution(mesh):
    return jax.shard_map(
        on_device,
        mesh=mesh,
        in_specs=(
            P(("rep", "shard"), None, None),
            P("rep", "shard", None),
            P("shard", None),
            P("shard"),
            P("rep", "shard"),
            P("rep", "shard"),
            P(("rep", "shard"), None),
            P(),
            P(),
            P(),
            P(),
            P(("rep", "shard"), None),
        ),
        out_specs=(P("shard", None), P("shard"), P(("rep", "shard"))),
        check_vma=False,
    )
```

```python
import functools

import jax
import jax.numpy as jnp
from jax import lax
from jax.experimental import pallas as pl
from jax.experimental.pallas import tpu as pltpu
from jax.sharding import PartitionSpec as P

MESH = pl.DeviceIdType.MESH
BLOCK = 128
NS = 32
NR = 16
NY = 8
LEARN = 0.5
BF = jnp.bfloat16
F32 = jnp.float32


def remote(src, dst, send, recv, rep, shard):
    return pltpu.make_async_remote_copy(
        src_ref=src,
        dst_ref=dst,
        send_sem=send,
        recv_sem=recv,
        device_id={"rep": rep, "shard": shard},
        device_id_type=MESH,
    )


def matmul(a, b):
    return jnp.dot(a, b, preferred_element_type=F32)


def matmul_nt(a, b):
    return lax.dot_general(a, b, (((1,), (1,)), ((), ())), preferred_element_type=F32)


def matmul_tn(a, b):
    return lax.dot_general(a, b, (((0,), (0,)), ((), ())), preferred_element_type=F32)


def exchange(
    pooled_in,
    ids_in,
    accum_in,
    listed_in,
    counts_in,
    xz_in,
    w_top_in,
    u_proj_in,
    v_proj_in,
    bias_in,
    d_act_in,
    rows_hbm,
    stats_hbm,
    blocks_hbm,
    dense_hbm,
    rows_out,
    stats_out,
    blocks_out,
    dense_out,
    out_sem,
    pooled,
    ids,
    accum,
    listed,
    counts,
    xz,
    w_top,
    u_proj,
    v_proj,
    bias,
    d_act,
    in_sem,
    wide,
    a_src,
    a_dst,
    hits,
    hid_all,
    right,
    cols,
    l_dst,
    x_dst,
    part,
    part_dst,
    a_send,
    a_recv,
    l_send,
    l_recv,
    x_send,
    x_recv,
    own_sem,
    c_send,
    c_recv,
    st_send,
    st_recv,
    p_send,
    p_recv,
):
    rep = lax.axis_index("rep")
    shard = lax.axis_index("shard")

    samples, feats, width = pooled.shape
    chunk = samples // 4
    pairs = tuple((pooled_in.at[pl.ds(i * chunk, chunk)], pooled.at[pl.ds(i * chunk, chunk)]) for i in range(4)) + (
        (xz_in, xz),
        (v_proj_in, v_proj),
        (u_proj_in, u_proj),
        (bias_in, bias),
        (w_top_in, w_top),
        (d_act_in, d_act),
        (listed_in, listed),
        (counts_in, counts),
        (ids_in, ids),
        (accum_in, accum),
    )
    fetched = [pltpu.make_async_copy(src, dst, in_sem.at[i]) for i, (src, dst) in enumerate(pairs)]
    for copy in fetched:
        copy.start()

    barrier = pltpu.get_barrier_semaphore()

    @pl.loop(1, NS)
    def _(p):
        pl.semaphore_signal(
            barrier, inc=1, device_id={"rep": rep, "shard": lax.rem(shard + p, NS)}, device_id_type=MESH
        )

    @pl.loop(1, NR)
    def _(p):
        pl.semaphore_signal(
            barrier, inc=1, device_id={"rep": lax.rem(rep + p, NR), "shard": shard}, device_id_type=MESH
        )

    for i in range(4):
        fetched[i].wait()
        taken = pooled[i * chunk : (i + 1) * chunk].astype(F32).reshape(chunk * feats, width)
        wide[0, pl.ds(i * chunk * feats, chunk * feats), :] = taken[:, :128]
        wide[1, pl.ds(i * chunk * feats, chunk * feats), :] = taken[:, 128:]

    pl.semaphore_wait(barrier, NS + NR - 2)

    stored = []

    def store(src, dst):
        copy = pltpu.make_async_copy(src, dst, out_sem.at[len(stored)])
        copy.start()
        stored.append(copy)

    y = rep // 2
    xl = lax.rem(rep, 2)

    def at(dy, flip):
        return lax.rem(y + dy + NY, NY) * 2 + ((1 - xl) if flip else xl)

    across = at(0, True)

    class Gather:
        def __init__(self, ref, send, recv, diagonal, out=None):
            self.ref, self.send, self.recv, self.diagonal, self.out = ref, send, recv, diagonal, out
            self.copies = []

        def view(self, ref, q, half):
            if half is None:
                return ref.at[q]
            rows = ref.shape[1] // 2
            return ref.at[q, pl.ds(half * rows, rows)]

        def start(self, q, to, half=None):
            ref = self.view(self.ref, q, half)
            copy = remote(ref, ref, self.send.at[len(self.copies)], self.recv.at[q, half or 0], to, shard)
            copy.start()
            self.copies.append(copy)

        def wait(self, q, half=None):
            ref = self.view(self.ref, q, half)
            remote(ref, ref, self.send.at[0], self.recv.at[q, half or 0], across, shard).wait_recv()
            if self.out is not None:
                store(ref, self.view(self.out, q, half))

        def begin(self):
            for to in (at(2, False), at(-2, False), at(1, False), at(-1, False), across):
                self.start(rep, to)

        def middle(self):
            for side, half in ((1, 0), (-1, 1)):
                q = at(-2 * side, False)
                self.wait(q)
                self.start(q, at(2 * side, False), half)
                self.start(q, at(side, False))
                if self.diagonal:
                    self.start(q, at(side, True))
                self.start(q, across)
            self.wait(across)
            for side in (1, -1):
                self.start(across, at(side, False))

        def late(self):
            for dy in (-3, 3):
                self.wait(at(dy, False))
                if not self.diagonal:
                    self.start(at(dy, False), across)
            for half in (0, 1):
                self.wait(at(4, False), half)
                self.start(at(4, False), across, half)

        def end(self):
            for dy in (-1, 1):
                self.wait(at(dy, False))
            for dy in (-1, 1, -2, 2, -3, 3):
                self.wait(at(dy, True))
            for half in (0, 1):
                self.wait(at(4, True), half)

        def drain(self):
            for copy in self.copies:
                copy.wait_send()

    x_gather = Gather(x_dst, x_send, x_recv, True)
    row_gathers = (
        Gather(rows_out.at[0], c_send.at[0], c_recv.at[0], False),
        Gather(rows_out.at[1], c_send.at[1], c_recv.at[1], True, rows_hbm.at[1]),
    )

    def pick(h, f):
        return wide[h, pl.ds(f, samples, stride=feats), :].astype(BF)

    def a_out(h, p):
        t = lax.rem(shard + p, NS)
        return remote(a_src.at[h, t], a_dst.at[h, shard], a_send.at[h, p], a_recv.at[h, shard], rep, t)

    def a_in(h, p):
        t = lax.rem(shard + p, NS)
        return remote(a_src.at[h, t], a_dst.at[h, t], a_send.at[h, p], a_recv.at[h, t], rep, t)

    @pl.loop(1, NS)
    def _(p):
        t = lax.rem(shard + p, NS)
        a_src[0, t] = pick(0, t)
        a_out(0, p).start()

    def l_copy(p, slot):
        t = lax.rem(rep + p, NR)
        at = pl.multiple_of(((5 * t) // 4) * 128, 128)
        return remote(cols.at[:, pl.ds(at, 256)], l_dst.at[slot(t)], l_send.at[p], l_recv.at[slot(t)], t, shard)

    mine, theirs = (lambda t: rep), (lambda t: t)

    fetched[4].wait()
    x = xz[...]
    x_dst[rep] = x
    x_gather.begin()
    for copy in fetched[5:]:
        copy.wait()
    x_wide = x.astype(F32)
    hid = matmul(x, v_proj[...]).astype(BF)
    mixed = matmul_nt(hid, u_proj[...]) + bias[...]
    x_one = (x_wide * mixed + x_wide).astype(BF)
    hidden = d_act.shape[1]
    back = jnp.zeros((samples, width), F32)
    for c in range(0, hidden, 512):
        z = matmul(x_one, w_top[:, c : c + 512])
        sig = jax.nn.sigmoid(z)
        dz = (d_act[:, c : c + 512].astype(F32) * sig * (1.0 + z * (1.0 - sig))).astype(BF)
        cols[:, c : c + 512] = dz
        back = back + matmul_nt(dz, w_top[:, c : c + 512])
    dp = (back * x_wide).astype(BF)
    cols[:, hidden : hidden + width] = dp
    cols[:, hidden + width : hidden + 2 * width] = dp

    @pl.loop(1, NR)
    def _(p):
        l_copy(p, mine).start()

    own_at = pl.multiple_of(((5 * rep) // 4) * 128, 128)
    own_copy = pltpu.make_async_copy(cols.at[:, pl.ds(own_at, 256)], l_dst.at[rep], own_sem)
    own_copy.start()

    @pl.loop(1, NS)
    def _(p):
        t = lax.rem(shard + p, NS)
        a_src[1, t] = pick(1, t)
        a_out(1, p).start()

    for h in range(2):
        a_dst[h, shard] = pick(h, shard)

    x_gather.middle()

    slots = listed.shape[1]
    lookups = ids.shape[1]
    for k in range(slots):
        first = jnp.where(counts[0, 0] > k, listed[0, k] * BLOCK, -(1 << 20))
        for c in range(0, lookups, 512):
            rel = ids[:, c : c + 512] - first
            row = lax.broadcasted_iota(jnp.int32, (BLOCK, 512), 0)
            hit = jnp.zeros((BLOCK, 512), F32)
            for pos in range(ids.shape[0]):
                hit = hit + jnp.where(row == rel[pos : pos + 1, :], 1.0, 0.0)
            hits[k * BLOCK : (k + 1) * BLOCK, c : c + 512] = hit.astype(BF)

    def gradient(h):
        @pl.loop(1, NS)
        def _(p):
            a_in(h, p).wait_recv()

        grad = matmul(hits[...], a_dst[h].reshape(lookups, 128))
        rows_out[h, rep] = grad.astype(BF)
        row_gathers[h].begin()
        if h == 1:
            store(rows_out.at[h, rep], rows_hbm.at[h, rep])
        return jnp.sum(grad * grad, axis=1, keepdims=True)

    square = gradient(0)
    x_gather.late()
    row_gathers[0].middle()
    square = (square + gradient(1)) * (1.0 / width)

    diag = lax.broadcasted_iota(jnp.int32, (BLOCK, BLOCK), 0) == lax.broadcasted_iota(jnp.int32, (BLOCK, BLOCK), 1)
    change, scale, block = [], [], []
    for k in range(slots):
        col = jnp.broadcast_to(square[k * BLOCK : (k + 1) * BLOCK], (BLOCK, BLOCK))
        mean = jnp.sum(jnp.where(diag, col, 0.0), axis=0, keepdims=True)
        old = accum[pl.ds(listed[0, k], 1), :]
        change.append(mean)
        scale.append(LEARN * lax.rsqrt(old + mean))
        block.append(jnp.full((1, BLOCK), listed[0, k].astype(F32), F32))
    stats_out[rep] = jnp.concatenate(change + scale + block + [jnp.zeros((2, BLOCK), F32)], axis=0)

    def st_copy(p, slot):
        t = lax.rem(rep + p, NR)
        return remote(stats_out.at[slot(t)], stats_out.at[slot(t)], st_send.at[p], st_recv.at[slot(t)], t, shard)

    @pl.loop(1, NR)
    def _(p):
        st_copy(p, mine).start()

    row_gathers[0].late()
    x_gather.end()
    many = NR * samples
    xs = x_dst[...].reshape(many, width)
    hids = matmul(xs, v_proj[...]).astype(BF)
    hid_all[...] = hids

    @pl.when(rep <= 12)
    def _():
        wide_xs = x_dst[...].reshape(many, width).astype(F32)
        mixing = matmul_nt(hid_all[...], u_proj[...]) + bias[...]
        right[...] = (wide_xs * mixing + wide_xs).astype(BF)

    @pl.when(rep > 12)
    def _():
        right[...] = hid_all[...]

    row_gathers[1].middle()

    @pl.loop(1, NR)
    def _(p):
        l_copy(p, theirs).wait_recv()

    own_copy.wait()

    def spread(values, offset):
        source = lax.broadcasted_iota(jnp.int32, (width, width), 0)
        target = lax.broadcasted_iota(jnp.int32, (width, width), 1)
        chosen = (source == (target // 8) * 5 + target % 8 + offset) & (target % 8 < 5)
        return matmul(values, jnp.where(chosen, 1.0, 0.0).astype(BF)).astype(BF)

    line = lax.broadcasted_iota(jnp.int32, (width, width), 0)
    line = (line // 8) * 5 + line % 8

    @pl.when(rep < 15)
    def _():
        left = spread(l_dst[...].reshape(many, width), 32 * lax.rem(rep, 4))
        part[...] = matmul_tn(left, right[...]).reshape(NS, 8, width)

    @pl.when(rep == 12)
    def _():
        left = spread(l_dst[...].reshape(many, width), 0)
        below = matmul_tn(left, hid_all[...])
        part[...] = jnp.where(line < 128, part[...].reshape(width, width), below).reshape(NS, 8, width)

    @pl.when(rep >= 14)
    def _():
        ls = l_dst[...].reshape(many, width)
        low, high = u_proj[: width // 2, :], u_proj[width // 2 :, :]
        dhs = (
            matmul(ls[:, : width // 2], jnp.where(rep == 14, high, low))
            + matmul(ls[:, width // 2 :], jnp.where(rep == 14, low, high))
        ).astype(BF)
        left = spread(x_dst[...].reshape(many, width), jnp.where(rep == 14, -64, 96))
        below = matmul_tn(left, dhs)
        above = jnp.where(rep == 14, part[...].reshape(width, width), below)
        part[...] = jnp.where(line < 64, above, below).reshape(NS, 8, width)

    part_dst[shard] = part[shard]

    def p_copy(p, slot):
        t = lax.rem(shard + p, NS)
        return remote(part.at[t], part_dst.at[slot(t)], p_send.at[p], p_recv.at[slot(t)], rep, t)

    own_shard, that_shard = (lambda t: shard), (lambda t: t)

    @pl.loop(1, NS)
    def _(p):
        p_copy(p, own_shard).start()

    row_gathers[1].late()
    row_gathers[0].end()
    store(rows_out.at[0], rows_hbm.at[0])

    @pl.loop(1, NR)
    def _(p):
        st_copy(p, theirs).wait_recv()

    lane = lax.broadcasted_iota(jnp.int32, (1, BLOCK), 1)
    blocks = jnp.zeros((1, BLOCK), F32)
    for r in range(NR):
        for k in range(slots):
            row = stats_out[r, 2 * slots + k : 2 * slots + k + 1, :]
            blocks = blocks + jnp.where(lane == r * slots + k, row, 0.0)
    blocks_out[...] = blocks.astype(jnp.int32)
    store(stats_out, stats_hbm)
    store(blocks_out, blocks_hbm)
    row_gathers[1].end()

    @pl.loop(1, NS)
    def _(p):
        p_copy(p, that_shard).wait_recv()

    dense_out[...] = jnp.sum(part_dst[...], axis=0)
    store(dense_out, dense_hbm)

    @pl.loop(1, NS)
    def _(p):
        a_out(0, p).wait_send()
        a_out(1, p).wait_send()
        p_copy(p, own_shard).wait_send()

    @pl.loop(1, NR)
    def _(p):
        l_copy(p, mine).wait_send()
        st_copy(p, mine).wait_send()

    x_gather.drain()
    for gather in row_gathers:
        gather.drain()
    for copy in stored:
        copy.wait()


def apply(
    norm,
    blocks_in,
    table_in,
    accum_in,
    rows_in,
    stats_in,
    dense_in,
    table_out,
    accum_out,
    dense_out,
    blocks,
    table,
    accum,
    rows,
    stats,
    dense,
    done,
    total,
    state,
    sems,
    in_sems,
):
    nblk, block, width = table.shape
    reps = rows.shape[1]
    slots = 2
    groups = 4
    per = reps // groups
    pairs = [(blocks_in, blocks), (stats_in, stats)]
    pairs += [(rows_in.at[:, pl.ds(i * per, per)], rows.at[:, pl.ds(i * per, per)]) for i in range(groups)]
    pairs += [(table_in, table), (accum_in, accum), (dense_in, dense)]
    fetched = [pltpu.make_async_copy(src, dst, in_sems.at[i]) for i, (src, dst) in enumerate(pairs)]
    for copy in fetched:
        copy.start()
    total[...] = jnp.zeros_like(total)
    state[...] = jnp.zeros_like(state)
    fetched[0].wait()
    fetched[1].wait()
    scales = jnp.transpose(stats[...].reshape(reps * 8, block))
    for r in range(reps):
        if r % per == 0:
            fetched[2 + r // per].wait()
        for k in range(slots):
            b = blocks[0, r * slots + k]
            col = scales[:, r * 8 + slots + k : r * 8 + slots + k + 1]
            for h in range(2):
                g = rows[h, r, k * block : (k + 1) * block, :].astype(F32)
                total[b, :, h * 128 : (h + 1) * 128] += g * col
            state[pl.ds(b, 1), :] += stats[r, k : k + 1, :]
    for copy in fetched[2 + groups :]:
        copy.wait()
    step = nblk // groups
    stores = []
    for i in range(groups):
        for b in range(i * step, (i + 1) * step):
            done[b] = (table[b].astype(F32) - total[b] * (1.0 / reps)).astype(BF)
        at = pl.ds(i * step, step)
        stores.append(pltpu.make_async_copy(done.at[at], table_out.at[at], sems.at[i]))
        stores[-1].start()
    accum_out[...] = accum[...] + state[...] * (1.0 / reps)
    for j in range(5):
        for h in range(2):
            dense_out[2 * j + h : 2 * j + h + 1, :] = dense[j : j + 1, h * 128 : (h + 1) * 128] * norm
    for copy in stores:
        copy.wait()


def on_device(
    pooled_cot,
    bag_ids,
    table,
    accum,
    listed_block_index,
    counts,
    x_zero,
    w_top,
    u_proj,
    v_proj,
    cross_bias,
    d_act,
):
    width = table.shape[1]
    nblk = table.shape[0] // BLOCK
    samples, feats = pooled_cot.shape[:2]
    hidden = d_act.shape[1]
    slots = listed_block_index.shape[1]
    listed_rows = slots * BLOCK
    lookups = bag_ids.shape[0]
    vmem = pl.BlockSpec(memory_space=pltpu.VMEM)
    hbm = pl.BlockSpec(memory_space=pltpu.HBM)
    dma = pltpu.SemaphoreType.DMA
    ids = jnp.transpose(bag_ids.reshape(lookups, bag_ids.shape[2]))
    state = accum.reshape(nblk, BLOCK)
    rows, stats, blocks, dense = pl.pallas_call(
        exchange,
        out_shape=(
            jax.ShapeDtypeStruct((2, NR, listed_rows, 128), BF),
            jax.ShapeDtypeStruct((NR, 8, BLOCK), F32),
            jax.ShapeDtypeStruct((1, BLOCK), jnp.int32),
            jax.ShapeDtypeStruct((8, width), F32),
        ),
        in_specs=[hbm] * 11,
        out_specs=(hbm, hbm, hbm, hbm),
        scratch_shapes=[
            pltpu.VMEM((2, NR, listed_rows, 128), BF),
            pltpu.VMEM((NR, 8, BLOCK), F32),
            pltpu.VMEM((1, BLOCK), jnp.int32),
            pltpu.VMEM((8, width), F32),
            dma((24,)),
            pltpu.VMEM(pooled_cot.shape, BF),
            pltpu.VMEM(ids.shape, jnp.int32),
            pltpu.VMEM(state.shape, F32),
            pltpu.SMEM(listed_block_index.shape, jnp.int32),
            pltpu.SMEM(counts.shape, jnp.int32),
            pltpu.VMEM(x_zero.shape, BF),
            pltpu.VMEM(w_top.shape, BF),
            pltpu.VMEM(u_proj.shape, BF),
            pltpu.VMEM(v_proj.shape, BF),
            pltpu.VMEM((1, width), F32),
            pltpu.VMEM(d_act.shape, BF),
            dma((14,)),
            pltpu.VMEM((2, samples * feats, 128), F32),
            pltpu.VMEM((2, NS, samples, 128), BF),
            pltpu.VMEM((2, NS, samples, 128), BF),
            pltpu.VMEM((listed_rows, lookups), BF),
            pltpu.VMEM((NR * samples, width), BF),
            pltpu.VMEM((NR * samples, width), BF),
            pltpu.VMEM((samples, hidden + 2 * width), BF),
            pltpu.VMEM((NR, samples, width), BF),
            pltpu.VMEM((NR, samples, width), BF),
            pltpu.VMEM((NS, 8, width), F32),
            pltpu.VMEM((NS, 8, width), F32),
            dma((2, NS)),
            dma((2, NS)),
            dma((NR,)),
            dma((NR,)),
            dma((20,)),
            dma((NR, 2)),
            dma,
            dma((2, 20)),
            dma((2, NR, 2)),
            dma((NR,)),
            dma((NR,)),
            dma((NS,)),
            dma((NS,)),
        ],
        compiler_params=pltpu.CompilerParams(
            collective_id=0, has_side_effects=True, vmem_limit_bytes=60 << 20
        ),
        name="exchange",
    )(
        pooled_cot,
        ids,
        state,
        listed_block_index,
        counts,
        x_zero,
        w_top,
        u_proj,
        v_proj,
        cross_bias.reshape(1, width),
        d_act,
    )
    total = samples * lax.axis_size("rep") * lax.axis_size("shard")
    new_table, new_accum, out = pl.pallas_call(
        functools.partial(apply, float(total) ** -0.5),
        out_shape=(
            jax.ShapeDtypeStruct((nblk, BLOCK, width), BF),
            jax.ShapeDtypeStruct((nblk, BLOCK), F32),
            jax.ShapeDtypeStruct((10, 128), F32),
        ),
        in_specs=[hbm] * 6,
        out_specs=(hbm, vmem, vmem),
        scratch_shapes=[
            pltpu.SMEM((1, BLOCK), jnp.int32),
            pltpu.VMEM((nblk, BLOCK, width), BF),
            pltpu.VMEM((nblk, BLOCK), F32),
            pltpu.VMEM((2, NR, listed_rows, 128), BF),
            pltpu.VMEM((NR, 8, BLOCK), F32),
            pltpu.VMEM((8, width), F32),
            pltpu.VMEM((nblk, BLOCK, width), BF),
            pltpu.VMEM((nblk, BLOCK, width), F32),
            pltpu.VMEM((nblk, BLOCK), F32),
            dma((4,)),
            dma((9,)),
        ],
        compiler_params=pltpu.CompilerParams(vmem_limit_bytes=60 << 20),
        name="apply",
    )(blocks, table.reshape(nblk, BLOCK, width), state, rows, stats, dense)
    return (new_table.reshape(table.shape), new_accum.reshape(accum.shape), out.reshape(1280))


def solution(mesh):
    return jax.shard_map(
        on_device,
        mesh=mesh,
        in_specs=(
            P(("rep", "shard"), None, None),
            P("rep", "shard", None),
            P("shard", None),
            P("shard"),
            P("rep", "shard"),
            P("rep", "shard"),
            P(("rep", "shard"), None),
            P(),
            P(),
            P(),
            P(),
            P(("rep", "shard"), None),
        ),
        out_specs=(P("shard", None), P("shard"), P(("rep", "shard"))),
        check_vma=False,
    )
```

```python
import functools

import jax
import jax.numpy as jnp
from jax import lax
from jax.experimental import pallas as pl
from jax.experimental.pallas import tpu as pltpu
from jax.sharding import PartitionSpec as P

MESH = pl.DeviceIdType.MESH
BLOCK = 128
NS = 32
NR = 16
NY = 8
LEARN = 0.5
BF = jnp.bfloat16
F32 = jnp.float32


def remote(src, dst, send, recv, rep, shard):
    return pltpu.make_async_remote_copy(
        src_ref=src,
        dst_ref=dst,
        send_sem=send,
        recv_sem=recv,
        device_id={"rep": rep, "shard": shard},
        device_id_type=MESH,
    )


def matmul(a, b):
    return jnp.dot(a, b, preferred_element_type=F32)


def matmul_nt(a, b):
    return lax.dot_general(a, b, (((1,), (1,)), ((), ())), preferred_element_type=F32)


def matmul_tn(a, b):
    return lax.dot_general(a, b, (((0,), (0,)), ((), ())), preferred_element_type=F32)


def exchange(
    pooled_in,
    ids_in,
    accum_in,
    listed_in,
    counts_in,
    xz_in,
    w_top_in,
    u_proj_in,
    v_proj_in,
    bias_in,
    d_act_in,
    rows_hbm,
    stats_hbm,
    blocks_hbm,
    dense_hbm,
    rows_out,
    stats_out,
    blocks_out,
    dense_out,
    out_sem,
    pooled,
    ids,
    accum,
    listed,
    counts,
    xz,
    w_top,
    u_proj,
    v_proj,
    bias,
    d_act,
    in_sem,
    wide,
    a_src,
    a_dst,
    hits,
    hid_all,
    right,
    cols,
    l_dst,
    x_dst,
    part,
    part_src,
    part_dst,
    a_send,
    a_recv,
    l_send,
    l_recv,
    x_send,
    x_recv,
    own_sem,
    c_send,
    c_recv,
    st_send,
    st_recv,
    p_send,
    p_recv,
):
    rep = lax.axis_index("rep")
    shard = lax.axis_index("shard")

    samples, feats, width = pooled.shape
    chunk = samples // 4
    pairs = tuple((pooled_in.at[pl.ds(i * chunk, chunk)], pooled.at[pl.ds(i * chunk, chunk)]) for i in range(4)) + (
        (xz_in, xz),
        (v_proj_in, v_proj),
        (u_proj_in, u_proj),
        (bias_in, bias),
        (w_top_in, w_top),
        (d_act_in, d_act),
        (listed_in, listed),
        (counts_in, counts),
        (ids_in, ids),
        (accum_in, accum),
    )
    fetched = [pltpu.make_async_copy(src, dst, in_sem.at[i]) for i, (src, dst) in enumerate(pairs)]
    for copy in fetched[:4]:
        copy.start()

    barrier = pltpu.get_barrier_semaphore()

    @pl.loop(1, NS)
    def _(p):
        pl.semaphore_signal(
            barrier, inc=1, device_id={"rep": rep, "shard": lax.rem(shard + p, NS)}, device_id_type=MESH
        )

    @pl.loop(1, NR)
    def _(p):
        pl.semaphore_signal(
            barrier, inc=1, device_id={"rep": lax.rem(rep + p, NR), "shard": shard}, device_id_type=MESH
        )

    for i in range(4):
        fetched[i].wait()
        taken = pooled[i * chunk : (i + 1) * chunk].astype(F32).reshape(chunk * feats, width)
        wide[0, pl.ds(i * chunk * feats, chunk * feats), :] = taken[:, :128]
        wide[1, pl.ds(i * chunk * feats, chunk * feats), :] = taken[:, 128:]

    pl.semaphore_wait(barrier, NS + NR - 2)

    stored = []

    def store(src, dst):
        copy = pltpu.make_async_copy(src, dst, out_sem.at[len(stored)])
        copy.start()
        stored.append(copy)

    y = rep // 2
    xl = lax.rem(rep, 2)

    def at(dy, flip):
        return lax.rem(y + dy + NY, NY) * 2 + ((1 - xl) if flip else xl)

    across = at(0, True)

    class Gather:
        def __init__(self, ref, send, recv, diagonal, out=None):
            self.ref, self.send, self.recv, self.diagonal, self.out = ref, send, recv, diagonal, out
            self.copies = []

        def view(self, ref, q, half):
            if half is None:
                return ref.at[q]
            rows = ref.shape[1] // 2
            return ref.at[q, pl.ds(half * rows, rows)]

        def start(self, q, to, half=None):
            ref = self.view(self.ref, q, half)
            copy = remote(ref, ref, self.send.at[len(self.copies)], self.recv.at[q, half or 0], to, shard)
            copy.start()
            self.copies.append(copy)

        def wait(self, q, half=None):
            ref = self.view(self.ref, q, half)
            remote(ref, ref, self.send.at[0], self.recv.at[q, half or 0], across, shard).wait_recv()
            if self.out is not None:
                store(ref, self.view(self.out, q, half))

        def begin(self):
            for to in (at(2, False), at(-2, False), at(1, False), at(-1, False), across):
                self.start(rep, to)

        def middle(self):
            for side, half in ((1, 0), (-1, 1)):
                q = at(-2 * side, False)
                self.wait(q)
                self.start(q, at(2 * side, False), half)
                self.start(q, at(side, False))
                if self.diagonal:
                    self.start(q, at(side, True))
                self.start(q, across)
            self.wait(across)
            for side in (1, -1):
                self.start(across, at(side, False))

        def late(self):
            for dy in (-3, 3):
                self.wait(at(dy, False))
                if not self.diagonal:
                    self.start(at(dy, False), across)
            for half in (0, 1):
                self.wait(at(4, False), half)
                self.start(at(4, False), across, half)

        def end(self):
            for dy in (-1, 1):
                self.wait(at(dy, False))
            for dy in (-1, 1, -2, 2, -3, 3):
                self.wait(at(dy, True))
            for half in (0, 1):
                self.wait(at(4, True), half)

        def drain(self):
            for copy in self.copies:
                copy.wait_send()

    x_gather = Gather(x_dst, x_send, x_recv, True)
    row_gathers = (
        Gather(rows_out.at[0], c_send.at[0], c_recv.at[0], True),
        Gather(rows_out.at[1], c_send.at[1], c_recv.at[1], True, rows_hbm.at[1]),
    )

    def pick(h, f):
        return wide[h, pl.ds(f, samples, stride=feats), :].astype(BF)

    def a_out(h, p):
        t = lax.rem(shard + p, NS)
        return remote(a_src.at[h, t], a_dst.at[h, shard], a_send.at[h, p], a_recv.at[h, shard], rep, t)

    def a_in(h, p):
        t = lax.rem(shard + p, NS)
        return remote(a_src.at[h, t], a_dst.at[h, t], a_send.at[h, p], a_recv.at[h, t], rep, t)

    @pl.loop(1, NS)
    def _(p):
        t = lax.rem(shard + p, NS)
        a_src[0, t] = pick(0, t)
        a_out(0, p).start()

    def l_copy(p, slot):
        t = lax.rem(rep + p, NR)
        at = pl.multiple_of(((5 * t) // 4) * 128, 128)
        return remote(cols.at[:, pl.ds(at, 256)], l_dst.at[slot(t)], l_send.at[p], l_recv.at[slot(t)], t, shard)

    mine, theirs = (lambda t: rep), (lambda t: t)

    for copy in fetched[4:]:
        copy.start()
    fetched[4].wait()
    x = xz[...]
    x_dst[rep] = x
    x_gather.begin()
    for copy in fetched[5:]:
        copy.wait()
    x_wide = x.astype(F32)
    hid = matmul(x, v_proj[...]).astype(BF)
    mixed = matmul_nt(hid, u_proj[...]) + bias[...]
    x_one = (x_wide * mixed + x_wide).astype(BF)
    hidden = d_act.shape[1]
    back = jnp.zeros((samples, width), F32)
    for c in range(0, hidden, 512):
        z = matmul(x_one, w_top[:, c : c + 512])
        sig = jax.nn.sigmoid(z)
        dz = (d_act[:, c : c + 512].astype(F32) * sig * (1.0 + z * (1.0 - sig))).astype(BF)
        cols[:, c : c + 512] = dz
        back = back + matmul_nt(dz, w_top[:, c : c + 512])
    dp = (back * x_wide).astype(BF)
    cols[:, hidden : hidden + width] = dp
    cols[:, hidden + width : hidden + 2 * width] = dp

    @pl.loop(1, NR)
    def _(p):
        l_copy(p, mine).start()

    own_at = pl.multiple_of(((5 * rep) // 4) * 128, 128)
    own_copy = pltpu.make_async_copy(cols.at[:, pl.ds(own_at, 256)], l_dst.at[rep], own_sem)
    own_copy.start()

    @pl.loop(1, NS)
    def _(p):
        t = lax.rem(shard + p, NS)
        a_src[1, t] = pick(1, t)
        a_out(1, p).start()

    for h in range(2):
        a_dst[h, shard] = pick(h, shard)

    x_gather.middle()

    slots = listed.shape[1]
    lookups = ids.shape[1]
    for k in range(slots):
        first = jnp.where(counts[0, 0] > k, listed[0, k] * BLOCK, -(1 << 20))
        for c in range(0, lookups, 512):
            rel = ids[:, c : c + 512] - first
            row = lax.broadcasted_iota(jnp.int32, (BLOCK, 512), 0)
            hit = jnp.zeros((BLOCK, 512), F32)
            for pos in range(ids.shape[0]):
                hit = hit + jnp.where(row == rel[pos : pos + 1, :], 1.0, 0.0)
            hits[k * BLOCK : (k + 1) * BLOCK, c : c + 512] = hit.astype(BF)

    def gradient(h):
        @pl.loop(1, NS)
        def _(p):
            a_in(h, p).wait_recv()

        grad = matmul(hits[...], a_dst[h].reshape(lookups, 128))
        rows_out[h, rep] = grad.astype(BF)
        row_gathers[h].begin()
        if h == 1:
            store(rows_out.at[h, rep], rows_hbm.at[h, rep])
        return jnp.sum(grad * grad, axis=1, keepdims=True)

    square = gradient(0)
    x_gather.late()
    row_gathers[0].middle()
    square = (square + gradient(1)) * (1.0 / width)

    diag = lax.broadcasted_iota(jnp.int32, (BLOCK, BLOCK), 0) == lax.broadcasted_iota(jnp.int32, (BLOCK, BLOCK), 1)
    change, scale, block = [], [], []
    for k in range(slots):
        col = jnp.broadcast_to(square[k * BLOCK : (k + 1) * BLOCK], (BLOCK, BLOCK))
        mean = jnp.sum(jnp.where(diag, col, 0.0), axis=0, keepdims=True)
        old = accum[pl.ds(listed[0, k], 1), :]
        change.append(mean)
        scale.append(LEARN * lax.rsqrt(old + mean))
        block.append(jnp.full((1, BLOCK), listed[0, k].astype(F32), F32))
    stats_out[rep] = jnp.concatenate(change + scale + block + [jnp.zeros((2, BLOCK), F32)], axis=0)

    def st_copy(p, slot):
        t = lax.rem(rep + p, NR)
        return remote(stats_out.at[slot(t)], stats_out.at[slot(t)], st_send.at[p], st_recv.at[slot(t)], t, shard)

    @pl.loop(1, NR)
    def _(p):
        st_copy(p, mine).start()

    row_gathers[0].late()
    x_gather.end()
    many = NR * samples
    xs = x_dst[...].reshape(many, width)
    hids = matmul(xs, v_proj[...]).astype(BF)
    hid_all[...] = hids

    @pl.when(rep <= 12)
    def _():
        wide_xs = x_dst[...].reshape(many, width).astype(F32)
        mixing = matmul_nt(hid_all[...], u_proj[...]) + bias[...]
        right[...] = (wide_xs * mixing + wide_xs).astype(BF)

    @pl.when(rep > 12)
    def _():
        right[...] = hid_all[...]

    row_gathers[1].middle()

    @pl.loop(1, NR)
    def _(p):
        l_copy(p, theirs).wait_recv()

    own_copy.wait()

    def spread(values, offset):
        source = lax.broadcasted_iota(jnp.int32, (width, width), 0)
        target = lax.broadcasted_iota(jnp.int32, (1, width), 1)
        group, place = target >> 3, target & 7
        chosen = source == jnp.where(place < 5, group * 5 + place + offset, -1)
        return matmul(values, jnp.where(chosen, 1.0, 0.0).astype(BF)).astype(BF)

    line = lax.broadcasted_iota(jnp.int32, (width, width), 0)
    line = (line >> 3) * 5 + (line & 7)

    @pl.when(rep < 15)
    def _():
        left = spread(l_dst[...].reshape(many, width), 32 * lax.rem(rep, 4))
        part[...] = matmul_tn(left, right[...]).reshape(NS, 8, width)

    @pl.when(rep == 12)
    def _():
        left = spread(l_dst[...].reshape(many, width), 0)
        below = matmul_tn(left, hid_all[...])
        part[...] = jnp.where(line < 128, part[...].reshape(width, width), below).reshape(NS, 8, width)

    @pl.when(rep >= 14)
    def _():
        ls = l_dst[...].reshape(many, width)
        low, high = u_proj[: width // 2, :], u_proj[width // 2 :, :]
        dhs = (
            matmul(ls[:, : width // 2], jnp.where(rep == 14, high, low))
            + matmul(ls[:, width // 2 :], jnp.where(rep == 14, low, high))
        ).astype(BF)
        left = spread(x_dst[...].reshape(many, width), jnp.where(rep == 14, -64, 96))
        below = matmul_tn(left, dhs)
        above = jnp.where(rep == 14, part[...].reshape(width, width), below)
        part[...] = jnp.where(line < 64, above, below).reshape(NS, 8, width)

    part_src[...] = jnp.concatenate([part[:, :, :128], part[:, :, 128:]], axis=1).astype(BF)
    part_dst[shard] = part_src[shard]

    def p_copy(p, slot):
        t = lax.rem(shard + p, NS)
        return remote(part_src.at[t], part_dst.at[slot(t)], p_send.at[p], p_recv.at[slot(t)], rep, t)

    own_shard, that_shard = (lambda t: shard), (lambda t: t)

    @pl.loop(1, NS)
    def _(p):
        p_copy(p, own_shard).start()

    row_gathers[1].late()
    row_gathers[0].end()
    store(rows_out.at[0], rows_hbm.at[0])

    @pl.loop(1, NR)
    def _(p):
        st_copy(p, theirs).wait_recv()

    lane = lax.broadcasted_iota(jnp.int32, (1, BLOCK), 1)
    blocks = jnp.zeros((1, BLOCK), F32)
    for r in range(NR):
        for k in range(slots):
            row = stats_out[r, 2 * slots + k : 2 * slots + k + 1, :]
            blocks = blocks + jnp.where(lane == r * slots + k, row, 0.0)
    blocks_out[...] = blocks.astype(jnp.int32)
    store(stats_out, stats_hbm)
    store(blocks_out, blocks_hbm)

    @pl.loop(1, NS)
    def _(p):
        p_copy(p, that_shard).wait_recv()

    dense_out[...] = jnp.sum(part_dst[...].astype(F32), axis=0)
    store(dense_out, dense_hbm)
    row_gathers[1].end()


    @pl.loop(1, NS)
    def _(p):
        a_out(0, p).wait_send()
        a_out(1, p).wait_send()
        p_copy(p, own_shard).wait_send()

    @pl.loop(1, NR)
    def _(p):
        l_copy(p, mine).wait_send()
        st_copy(p, mine).wait_send()

    x_gather.drain()
    for gather in row_gathers:
        gather.drain()
    for copy in stored:
        copy.wait()


def apply(
    norm,
    blocks_in,
    table_in,
    accum_in,
    rows_in,
    stats_in,
    dense_in,
    table_out,
    accum_out,
    dense_out,
    blocks,
    table,
    accum,
    rows,
    stats,
    dense,
    done,
    total,
    state,
    sems,
    in_sems,
):
    nblk, block, width = table.shape
    reps = rows.shape[1]
    slots = 2
    groups = 4
    per = reps // groups
    pairs = [(blocks_in, blocks), (stats_in, stats)]
    pairs += [(rows_in.at[:, pl.ds(i * per, per)], rows.at[:, pl.ds(i * per, per)]) for i in range(groups)]
    pairs += [(table_in, table), (accum_in, accum), (dense_in, dense)]
    fetched = [pltpu.make_async_copy(src, dst, in_sems.at[i]) for i, (src, dst) in enumerate(pairs)]
    for copy in fetched:
        copy.start()
    total[...] = jnp.zeros_like(total)
    state[...] = jnp.zeros_like(state)
    fetched[0].wait()
    fetched[1].wait()
    scales = jnp.transpose(stats[...].reshape(reps * 8, block))
    for r in range(reps):
        if r % per == 0:
            fetched[2 + r // per].wait()
        for k in range(slots):
            b = blocks[0, r * slots + k]
            col = scales[:, r * 8 + slots + k : r * 8 + slots + k + 1]
            for h in range(2):
                g = rows[h, r, k * block : (k + 1) * block, :].astype(F32)
                total[b, :, h * 128 : (h + 1) * 128] += g * col
            state[pl.ds(b, 1), :] += stats[r, k : k + 1, :]
    for copy in fetched[2 + groups :]:
        copy.wait()
    step = nblk // groups
    stores = []
    for i in range(groups):
        for b in range(i * step, (i + 1) * step):
            done[b] = (table[b].astype(F32) - total[b] * (1.0 / reps)).astype(BF)
        at = pl.ds(i * step, step)
        stores.append(pltpu.make_async_copy(done.at[at], table_out.at[at], sems.at[i]))
        stores[-1].start()
    accum_out[...] = accum[...] + state[...] * (1.0 / reps)
    for j in range(5):
        for h in range(2):
            dense_out[2 * j + h : 2 * j + h + 1, :] = dense[8 * h + j : 8 * h + j + 1, :] * norm
    for copy in stores:
        copy.wait()


def on_device(
    pooled_cot,
    bag_ids,
    table,
    accum,
    listed_block_index,
    counts,
    x_zero,
    w_top,
    u_proj,
    v_proj,
    cross_bias,
    d_act,
):
    width = table.shape[1]
    nblk = table.shape[0] // BLOCK
    samples, feats = pooled_cot.shape[:2]
    hidden = d_act.shape[1]
    slots = listed_block_index.shape[1]
    listed_rows = slots * BLOCK
    lookups = bag_ids.shape[0]
    vmem = pl.BlockSpec(memory_space=pltpu.VMEM)
    hbm = pl.BlockSpec(memory_space=pltpu.HBM)
    dma = pltpu.SemaphoreType.DMA
    ids = jnp.transpose(bag_ids.reshape(lookups, bag_ids.shape[2]))
    state = accum.reshape(nblk, BLOCK)
    rows, stats, blocks, dense = pl.pallas_call(
        exchange,
        out_shape=(
            jax.ShapeDtypeStruct((2, NR, listed_rows, 128), BF),
            jax.ShapeDtypeStruct((NR, 8, BLOCK), F32),
            jax.ShapeDtypeStruct((1, BLOCK), jnp.int32),
            jax.ShapeDtypeStruct((16, 128), F32),
        ),
        in_specs=[hbm] * 11,
        out_specs=(hbm, hbm, hbm, hbm),
        scratch_shapes=[
            pltpu.VMEM((2, NR, listed_rows, 128), BF),
            pltpu.VMEM((NR, 8, BLOCK), F32),
            pltpu.VMEM((1, BLOCK), jnp.int32),
            pltpu.VMEM((16, 128), F32),
            dma((24,)),
            pltpu.VMEM(pooled_cot.shape, BF),
            pltpu.VMEM(ids.shape, jnp.int32),
            pltpu.VMEM(state.shape, F32),
            pltpu.SMEM(listed_block_index.shape, jnp.int32),
            pltpu.SMEM(counts.shape, jnp.int32),
            pltpu.VMEM(x_zero.shape, BF),
            pltpu.VMEM(w_top.shape, BF),
            pltpu.VMEM(u_proj.shape, BF),
            pltpu.VMEM(v_proj.shape, BF),
            pltpu.VMEM((1, width), F32),
            pltpu.VMEM(d_act.shape, BF),
            dma((14,)),
            pltpu.VMEM((2, samples * feats, 128), F32),
            pltpu.VMEM((2, NS, samples, 128), BF),
            pltpu.VMEM((2, NS, samples, 128), BF),
            pltpu.VMEM((listed_rows, lookups), BF),
            pltpu.VMEM((NR * samples, width), BF),
            pltpu.VMEM((NR * samples, width), BF),
            pltpu.VMEM((samples, hidden + 2 * width), BF),
            pltpu.VMEM((NR, samples, width), BF),
            pltpu.VMEM((NR, samples, width), BF),
            pltpu.VMEM((NS, 8, width), F32),
            pltpu.VMEM((NS, 16, 128), BF),
            pltpu.VMEM((NS, 16, 128), BF),
            dma((2, NS)),
            dma((2, NS)),
            dma((NR,)),
            dma((NR,)),
            dma((20,)),
            dma((NR, 2)),
            dma,
            dma((2, 20)),
            dma((2, NR, 2)),
            dma((NR,)),
            dma((NR,)),
            dma((NS,)),
            dma((NS,)),
        ],
        compiler_params=pltpu.CompilerParams(
            collective_id=0, has_side_effects=True, vmem_limit_bytes=60 << 20
        ),
        name="exchange",
    )(
        pooled_cot,
        ids,
        state,
        listed_block_index,
        counts,
        x_zero,
        w_top,
        u_proj,
        v_proj,
        cross_bias.reshape(1, width),
        d_act,
    )
    total = samples * lax.axis_size("rep") * lax.axis_size("shard")
    new_table, new_accum, out = pl.pallas_call(
        functools.partial(apply, float(total) ** -0.5),
        out_shape=(
            jax.ShapeDtypeStruct((nblk, BLOCK, width), BF),
            jax.ShapeDtypeStruct((nblk, BLOCK), F32),
            jax.ShapeDtypeStruct((10, 128), F32),
        ),
        in_specs=[hbm] * 6,
        out_specs=(hbm, vmem, vmem),
        scratch_shapes=[
            pltpu.SMEM((1, BLOCK), jnp.int32),
            pltpu.VMEM((nblk, BLOCK, width), BF),
            pltpu.VMEM((nblk, BLOCK), F32),
            pltpu.VMEM((2, NR, listed_rows, 128), BF),
            pltpu.VMEM((NR, 8, BLOCK), F32),
            pltpu.VMEM((16, 128), F32),
            pltpu.VMEM((nblk, BLOCK, width), BF),
            pltpu.VMEM((nblk, BLOCK, width), F32),
            pltpu.VMEM((nblk, BLOCK), F32),
            dma((4,)),
            dma((9,)),
        ],
        compiler_params=pltpu.CompilerParams(vmem_limit_bytes=60 << 20),
        name="apply",
    )(blocks, table.reshape(nblk, BLOCK, width), state, rows, stats, dense)
    return (new_table.reshape(table.shape), new_accum.reshape(accum.shape), out.reshape(1280))


def solution(mesh):
    return jax.shard_map(
        on_device,
        mesh=mesh,
        in_specs=(
            P(("rep", "shard"), None, None),
            P("rep", "shard", None),
            P("shard", None),
            P("shard"),
            P("rep", "shard"),
            P("rep", "shard"),
            P(("rep", "shard"), None),
            P(),
            P(),
            P(),
            P(),
            P(("rep", "shard"), None),
        ),
        out_specs=(P("shard", None), P("shard"), P(("rep", "shard"))),
        check_vma=False,
    )
```

```python
import functools

import jax
import jax.numpy as jnp
from jax import lax
from jax.experimental import pallas as pl
from jax.experimental.pallas import tpu as pltpu
from jax.sharding import PartitionSpec as P

MESH = pl.DeviceIdType.MESH
BLOCK = 128
NS = 32
NR = 16
NY = 8
LEARN = 0.5
BF = jnp.bfloat16
F32 = jnp.float32


def remote(src, dst, send, recv, rep, shard):
    return pltpu.make_async_remote_copy(
        src_ref=src,
        dst_ref=dst,
        send_sem=send,
        recv_sem=recv,
        device_id={"rep": rep, "shard": shard},
        device_id_type=MESH,
    )


def matmul(a, b):
    return jnp.dot(a, b, preferred_element_type=F32)


def matmul_nt(a, b):
    return lax.dot_general(a, b, (((1,), (1,)), ((), ())), preferred_element_type=F32)


def matmul_tn(a, b):
    return lax.dot_general(a, b, (((0,), (0,)), ((), ())), preferred_element_type=F32)


def exchange(
    pooled_in,
    ids_in,
    accum_in,
    listed_in,
    counts_in,
    xz_in,
    w_top_in,
    u_proj_in,
    v_proj_in,
    bias_in,
    d_act_in,
    rows_hbm,
    stats_hbm,
    blocks_hbm,
    dense_hbm,
    rows_out,
    stats_out,
    blocks_out,
    dense_out,
    out_sem,
    pooled,
    ids,
    accum,
    listed,
    counts,
    xz,
    w_top,
    u_proj,
    v_proj,
    bias,
    d_act,
    in_sem,
    wide,
    a_src,
    a_dst,
    hits,
    hid_all,
    right,
    cols,
    l_dst,
    x_dst,
    part,
    part_src,
    part_dst,
    a_send,
    a_recv,
    l_send,
    l_recv,
    x_send,
    x_recv,
    own_sem,
    c_send,
    c_recv,
    st_send,
    st_recv,
    p_send,
    p_recv,
):
    rep = lax.axis_index("rep")
    shard = lax.axis_index("shard")

    samples, feats, width = pooled.shape
    chunk = samples // 4
    pairs = tuple((pooled_in.at[pl.ds(i * chunk, chunk)], pooled.at[pl.ds(i * chunk, chunk)]) for i in range(4)) + (
        (xz_in, xz),
        (v_proj_in, v_proj),
        (u_proj_in, u_proj),
        (bias_in, bias),
        (w_top_in, w_top),
        (d_act_in, d_act),
        (listed_in, listed),
        (counts_in, counts),
        (ids_in, ids),
        (accum_in, accum),
    )
    fetched = [pltpu.make_async_copy(src, dst, in_sem.at[i]) for i, (src, dst) in enumerate(pairs)]
    for copy in fetched[:4]:
        copy.start()

    barrier = pltpu.get_barrier_semaphore()

    @pl.loop(1, NS)
    def _(p):
        pl.semaphore_signal(
            barrier, inc=1, device_id={"rep": rep, "shard": lax.rem(shard + p, NS)}, device_id_type=MESH
        )

    @pl.loop(1, NR)
    def _(p):
        pl.semaphore_signal(
            barrier, inc=1, device_id={"rep": lax.rem(rep + p, NR), "shard": shard}, device_id_type=MESH
        )

    for i in range(4):
        fetched[i].wait()
        taken = pooled[i * chunk : (i + 1) * chunk].astype(F32).reshape(chunk * feats, width)
        wide[0, pl.ds(i * chunk * feats, chunk * feats), :] = taken[:, :128]
        wide[1, pl.ds(i * chunk * feats, chunk * feats), :] = taken[:, 128:]

    pl.semaphore_wait(barrier, NS + NR - 2)

    stored = []

    def store(src, dst):
        copy = pltpu.make_async_copy(src, dst, out_sem.at[len(stored)])
        copy.start()
        stored.append(copy)

    y = rep // 2
    xl = lax.rem(rep, 2)

    def at(dy, flip):
        return lax.rem(y + dy + NY, NY) * 2 + ((1 - xl) if flip else xl)

    across = at(0, True)

    class Gather:
        def __init__(self, ref, send, recv, diagonal, out=None):
            self.ref, self.send, self.recv, self.diagonal, self.out = ref, send, recv, diagonal, out
            self.copies = []

        def view(self, ref, q, half):
            if half is None:
                return ref.at[q]
            rows = ref.shape[1] // 2
            return ref.at[q, pl.ds(half * rows, rows)]

        def start(self, q, to, half=None):
            ref = self.view(self.ref, q, half)
            copy = remote(ref, ref, self.send.at[len(self.copies)], self.recv.at[q, half or 0], to, shard)
            copy.start()
            self.copies.append(copy)

        def wait(self, q, half=None):
            ref = self.view(self.ref, q, half)
            remote(ref, ref, self.send.at[0], self.recv.at[q, half or 0], across, shard).wait_recv()
            if self.out is not None:
                store(ref, self.view(self.out, q, half))

        def begin(self):
            for to in (at(2, False), at(-2, False), at(1, False), at(-1, False), across):
                self.start(rep, to)

        def middle(self):
            for side, half in ((1, 0), (-1, 1)):
                q = at(-2 * side, False)
                self.wait(q)
                self.start(q, at(2 * side, False), half)
                self.start(q, at(side, False))
                if self.diagonal:
                    self.start(q, at(side, True))
                self.start(q, across)
            self.wait(across)
            for side in (1, -1):
                self.start(across, at(side, False))

        def late(self):
            for dy in (-3, 3):
                self.wait(at(dy, False))
                if not self.diagonal:
                    self.start(at(dy, False), across)
            for half in (0, 1):
                self.wait(at(4, False), half)
                self.start(at(4, False), across, half)

        def end(self):
            for dy in (-1, 1):
                self.wait(at(dy, False))
            for dy in (-1, 1, -2, 2, -3, 3):
                self.wait(at(dy, True))
            for half in (0, 1):
                self.wait(at(4, True), half)

        def drain(self):
            for copy in self.copies:
                copy.wait_send()

    x_gather = Gather(x_dst, x_send, x_recv, False)
    row_gathers = (
        Gather(rows_out.at[0], c_send.at[0], c_recv.at[0], False),
        Gather(rows_out.at[1], c_send.at[1], c_recv.at[1], False, rows_hbm.at[1]),
    )

    def pick(h, f):
        return wide[h, pl.ds(f, samples, stride=feats), :].astype(BF)

    def a_out(h, p):
        t = lax.rem(shard + p, NS)
        return remote(a_src.at[h, t], a_dst.at[h, shard], a_send.at[h, p], a_recv.at[h, shard], rep, t)

    def a_in(h, p):
        t = lax.rem(shard + p, NS)
        return remote(a_src.at[h, t], a_dst.at[h, t], a_send.at[h, p], a_recv.at[h, t], rep, t)

    @pl.loop(1, NS)
    def _(p):
        t = lax.rem(shard + p, NS)
        a_src[0, t] = pick(0, t)
        a_out(0, p).start()

    def l_copy(p, slot):
        t = lax.rem(rep + p, NR)
        at = pl.multiple_of(((5 * t) // 4) * 128, 128)
        return remote(cols.at[:, pl.ds(at, 256)], l_dst.at[slot(t)], l_send.at[p], l_recv.at[slot(t)], t, shard)

    mine, theirs = (lambda t: rep), (lambda t: t)

    for copy in fetched[4:]:
        copy.start()
    fetched[4].wait()
    x = xz[...]
    x_dst[rep] = x
    x_gather.begin()
    for copy in fetched[5:]:
        copy.wait()
    x_wide = x.astype(F32)
    hid = matmul(x, v_proj[...]).astype(BF)
    mixed = matmul_nt(hid, u_proj[...]) + bias[...]
    x_one = (x_wide * mixed + x_wide).astype(BF)
    hidden = d_act.shape[1]
    back = jnp.zeros((samples, width), F32)
    for c in range(0, hidden, 512):
        z = matmul(x_one, w_top[:, c : c + 512])
        sig = jax.nn.sigmoid(z)
        dz = (d_act[:, c : c + 512].astype(F32) * sig * (1.0 + z * (1.0 - sig))).astype(BF)
        cols[:, c : c + 512] = dz
        back = back + matmul_nt(dz, w_top[:, c : c + 512])
    dp = (back * x_wide).astype(BF)
    cols[:, hidden : hidden + width] = dp
    cols[:, hidden + width : hidden + 2 * width] = dp

    @pl.loop(1, NR)
    def _(p):
        l_copy(p, mine).start()

    own_at = pl.multiple_of(((5 * rep) // 4) * 128, 128)
    own_copy = pltpu.make_async_copy(cols.at[:, pl.ds(own_at, 256)], l_dst.at[rep], own_sem)
    own_copy.start()

    @pl.loop(1, NS)
    def _(p):
        t = lax.rem(shard + p, NS)
        a_src[1, t] = pick(1, t)
        a_out(1, p).start()

    for h in range(2):
        a_dst[h, shard] = pick(h, shard)

    x_gather.middle()

    slots = listed.shape[1]
    lookups = ids.shape[1]
    for k in range(slots):
        first = jnp.where(counts[0, 0] > k, listed[0, k] * BLOCK, -(1 << 20))
        for c in range(0, lookups, 512):
            rel = ids[:, c : c + 512] - first
            row = lax.broadcasted_iota(jnp.int32, (BLOCK, 512), 0)
            hit = jnp.zeros((BLOCK, 512), F32)
            for pos in range(ids.shape[0]):
                hit = hit + jnp.where(row == rel[pos : pos + 1, :], 1.0, 0.0)
            hits[k * BLOCK : (k + 1) * BLOCK, c : c + 512] = hit.astype(BF)

    def gradient(h):
        @pl.loop(1, NS)
        def _(p):
            a_in(h, p).wait_recv()

        grad = matmul(hits[...], a_dst[h].reshape(lookups, 128))
        rows_out[h, rep] = grad.astype(BF)
        row_gathers[h].begin()
        if h == 1:
            store(rows_out.at[h, rep], rows_hbm.at[h, rep])
        return jnp.sum(grad * grad, axis=1, keepdims=True)

    square = gradient(0)
    x_gather.late()
    row_gathers[0].middle()
    square = (square + gradient(1)) * (1.0 / width)

    diag = lax.broadcasted_iota(jnp.int32, (BLOCK, BLOCK), 0) == lax.broadcasted_iota(jnp.int32, (BLOCK, BLOCK), 1)
    change, scale, block = [], [], []
    for k in range(slots):
        col = jnp.broadcast_to(square[k * BLOCK : (k + 1) * BLOCK], (BLOCK, BLOCK))
        mean = jnp.sum(jnp.where(diag, col, 0.0), axis=0, keepdims=True)
        old = accum[pl.ds(listed[0, k], 1), :]
        change.append(mean)
        scale.append(LEARN * lax.rsqrt(old + mean))
        block.append(jnp.full((1, BLOCK), listed[0, k].astype(F32), F32))
    stats_out[rep] = jnp.concatenate(change + scale + block + [jnp.zeros((2, BLOCK), F32)], axis=0)

    def st_copy(p, slot):
        t = lax.rem(rep + p, NR)
        return remote(stats_out.at[slot(t)], stats_out.at[slot(t)], st_send.at[p], st_recv.at[slot(t)], t, shard)

    @pl.loop(1, NR)
    def _(p):
        st_copy(p, mine).start()

    row_gathers[0].late()
    x_gather.end()
    many = NR * samples
    xs = x_dst[...].reshape(many, width)
    hids = matmul(xs, v_proj[...]).astype(BF)
    hid_all[...] = hids

    @pl.when(rep <= 12)
    def _():
        wide_xs = x_dst[...].reshape(many, width).astype(F32)
        mixing = matmul_nt(hid_all[...], u_proj[...]) + bias[...]
        right[...] = (wide_xs * mixing + wide_xs).astype(BF)

    @pl.when(rep > 12)
    def _():
        right[...] = hid_all[...]

    row_gathers[1].middle()

    @pl.loop(1, NR)
    def _(p):
        l_copy(p, theirs).wait_recv()

    own_copy.wait()

    def spread(values, offset):
        source = lax.broadcasted_iota(jnp.int32, (width, width), 0)
        target = lax.broadcasted_iota(jnp.int32, (1, width), 1)
        group, place = target >> 3, target & 7
        chosen = source == jnp.where(place < 5, group * 5 + place + offset, -1)
        return matmul(values, jnp.where(chosen, 1.0, 0.0).astype(BF)).astype(BF)

    line = lax.broadcasted_iota(jnp.int32, (width, width), 0)
    line = (line >> 3) * 5 + (line & 7)

    @pl.when(rep < 15)
    def _():
        left = spread(l_dst[...].reshape(many, width), 32 * lax.rem(rep, 4))
        part[...] = matmul_tn(left, right[...]).reshape(NS, 8, width)

    @pl.when(rep == 12)
    def _():
        left = spread(l_dst[...].reshape(many, width), 0)
        below = matmul_tn(left, hid_all[...])
        part[...] = jnp.where(line < 128, part[...].reshape(width, width), below).reshape(NS, 8, width)

    @pl.when(rep >= 14)
    def _():
        ls = l_dst[...].reshape(many, width)
        low, high = u_proj[: width // 2, :], u_proj[width // 2 :, :]
        dhs = (
            matmul(ls[:, : width // 2], jnp.where(rep == 14, high, low))
            + matmul(ls[:, width // 2 :], jnp.where(rep == 14, low, high))
        ).astype(BF)
        left = spread(x_dst[...].reshape(many, width), jnp.where(rep == 14, -64, 96))
        below = matmul_tn(left, dhs)
        above = jnp.where(rep == 14, part[...].reshape(width, width), below)
        part[...] = jnp.where(line < 64, above, below).reshape(NS, 8, width)

    part_src[...] = jnp.concatenate([part[:, :, :128], part[:, :, 128:]], axis=1).astype(BF)
    part_dst[shard] = part_src[shard]

    def p_copy(p, slot):
        t = lax.rem(shard + p, NS)
        return remote(part_src.at[t], part_dst.at[slot(t)], p_send.at[p], p_recv.at[slot(t)], rep, t)

    own_shard, that_shard = (lambda t: shard), (lambda t: t)

    @pl.loop(1, NS)
    def _(p):
        p_copy(p, own_shard).start()

    row_gathers[1].late()
    row_gathers[0].end()
    store(rows_out.at[0], rows_hbm.at[0])

    @pl.loop(1, NR)
    def _(p):
        st_copy(p, theirs).wait_recv()

    lane = lax.broadcasted_iota(jnp.int32, (1, BLOCK), 1)
    blocks = jnp.zeros((1, BLOCK), F32)
    for r in range(NR):
        for k in range(slots):
            row = stats_out[r, 2 * slots + k : 2 * slots + k + 1, :]
            blocks = blocks + jnp.where(lane == r * slots + k, row, 0.0)
    blocks_out[...] = blocks.astype(jnp.int32)
    store(stats_out, stats_hbm)
    store(blocks_out, blocks_hbm)

    @pl.loop(1, NS)
    def _(p):
        p_copy(p, that_shard).wait_recv()

    dense_out[...] = jnp.sum(part_dst[...].astype(F32), axis=0)
    store(dense_out, dense_hbm)
    row_gathers[1].end()


    @pl.loop(1, NS)
    def _(p):
        a_out(0, p).wait_send()
        a_out(1, p).wait_send()
        p_copy(p, own_shard).wait_send()

    @pl.loop(1, NR)
    def _(p):
        l_copy(p, mine).wait_send()
        st_copy(p, mine).wait_send()

    x_gather.drain()
    for gather in row_gathers:
        gather.drain()
    for copy in stored:
        copy.wait()


def apply(
    norm,
    blocks_in,
    table_in,
    accum_in,
    rows_in,
    stats_in,
    dense_in,
    table_out,
    accum_out,
    dense_out,
    blocks,
    table,
    accum,
    rows,
    stats,
    dense,
    done,
    total,
    state,
    sems,
    in_sems,
):
    nblk, block, width = table.shape
    reps = rows.shape[1]
    slots = 2
    groups = 4
    per = reps // groups
    pairs = [(blocks_in, blocks), (stats_in, stats)]
    pairs += [(rows_in.at[:, pl.ds(i * per, per)], rows.at[:, pl.ds(i * per, per)]) for i in range(groups)]
    pairs += [(table_in, table), (accum_in, accum), (dense_in, dense)]
    fetched = [pltpu.make_async_copy(src, dst, in_sems.at[i]) for i, (src, dst) in enumerate(pairs)]
    for copy in fetched:
        copy.start()
    total[...] = jnp.zeros_like(total)
    state[...] = jnp.zeros_like(state)
    fetched[0].wait()
    fetched[1].wait()
    scales = jnp.transpose(stats[...].reshape(reps * 8, block))
    for r in range(reps):
        if r % per == 0:
            fetched[2 + r // per].wait()
        for k in range(slots):
            b = blocks[0, r * slots + k]
            col = scales[:, r * 8 + slots + k : r * 8 + slots + k + 1]
            for h in range(2):
                g = rows[h, r, k * block : (k + 1) * block, :].astype(F32)
                total[b, :, h * 128 : (h + 1) * 128] += g * col
            state[pl.ds(b, 1), :] += stats[r, k : k + 1, :]
    for copy in fetched[2 + groups :]:
        copy.wait()
    step = nblk // groups
    stores = []
    for i in range(groups):
        for b in range(i * step, (i + 1) * step):
            done[b] = (table[b].astype(F32) - total[b] * (1.0 / reps)).astype(BF)
        at = pl.ds(i * step, step)
        stores.append(pltpu.make_async_copy(done.at[at], table_out.at[at], sems.at[i]))
        stores[-1].start()
    accum_out[...] = accum[...] + state[...] * (1.0 / reps)
    for j in range(5):
        for h in range(2):
            dense_out[2 * j + h : 2 * j + h + 1, :] = dense[8 * h + j : 8 * h + j + 1, :] * norm
    for copy in stores:
        copy.wait()


def on_device(
    pooled_cot,
    bag_ids,
    table,
    accum,
    listed_block_index,
    counts,
    x_zero,
    w_top,
    u_proj,
    v_proj,
    cross_bias,
    d_act,
):
    width = table.shape[1]
    nblk = table.shape[0] // BLOCK
    samples, feats = pooled_cot.shape[:2]
    hidden = d_act.shape[1]
    slots = listed_block_index.shape[1]
    listed_rows = slots * BLOCK
    lookups = bag_ids.shape[0]
    vmem = pl.BlockSpec(memory_space=pltpu.VMEM)
    hbm = pl.BlockSpec(memory_space=pltpu.HBM)
    dma = pltpu.SemaphoreType.DMA
    ids = jnp.transpose(bag_ids.reshape(lookups, bag_ids.shape[2]))
    state = accum.reshape(nblk, BLOCK)
    rows, stats, blocks, dense = pl.pallas_call(
        exchange,
        out_shape=(
            jax.ShapeDtypeStruct((2, NR, listed_rows, 128), BF),
            jax.ShapeDtypeStruct((NR, 8, BLOCK), F32),
            jax.ShapeDtypeStruct((1, BLOCK), jnp.int32),
            jax.ShapeDtypeStruct((16, 128), F32),
        ),
        in_specs=[hbm] * 11,
        out_specs=(hbm, hbm, hbm, hbm),
        scratch_shapes=[
            pltpu.VMEM((2, NR, listed_rows, 128), BF),
            pltpu.VMEM((NR, 8, BLOCK), F32),
            pltpu.VMEM((1, BLOCK), jnp.int32),
            pltpu.VMEM((16, 128), F32),
            dma((24,)),
            pltpu.VMEM(pooled_cot.shape, BF),
            pltpu.VMEM(ids.shape, jnp.int32),
            pltpu.VMEM(state.shape, F32),
            pltpu.SMEM(listed_block_index.shape, jnp.int32),
            pltpu.SMEM(counts.shape, jnp.int32),
            pltpu.VMEM(x_zero.shape, BF),
            pltpu.VMEM(w_top.shape, BF),
            pltpu.VMEM(u_proj.shape, BF),
            pltpu.VMEM(v_proj.shape, BF),
            pltpu.VMEM((1, width), F32),
            pltpu.VMEM(d_act.shape, BF),
            dma((14,)),
            pltpu.VMEM((2, samples * feats, 128), F32),
            pltpu.VMEM((2, NS, samples, 128), BF),
            pltpu.VMEM((2, NS, samples, 128), BF),
            pltpu.VMEM((listed_rows, lookups), BF),
            pltpu.VMEM((NR * samples, width), BF),
            pltpu.VMEM((NR * samples, width), BF),
            pltpu.VMEM((samples, hidden + 2 * width), BF),
            pltpu.VMEM((NR, samples, width), BF),
            pltpu.VMEM((NR, samples, width), BF),
            pltpu.VMEM((NS, 8, width), F32),
            pltpu.VMEM((NS, 16, 128), BF),
            pltpu.VMEM((NS, 16, 128), BF),
            dma((2, NS)),
            dma((2, NS)),
            dma((NR,)),
            dma((NR,)),
            dma((20,)),
            dma((NR, 2)),
            dma,
            dma((2, 20)),
            dma((2, NR, 2)),
            dma((NR,)),
            dma((NR,)),
            dma((NS,)),
            dma((NS,)),
        ],
        compiler_params=pltpu.CompilerParams(
            collective_id=0, has_side_effects=True, vmem_limit_bytes=60 << 20
        ),
        name="exchange",
    )(
        pooled_cot,
        ids,
        state,
        listed_block_index,
        counts,
        x_zero,
        w_top,
        u_proj,
        v_proj,
        cross_bias.reshape(1, width),
        d_act,
    )
    total = samples * lax.axis_size("rep") * lax.axis_size("shard")
    new_table, new_accum, out = pl.pallas_call(
        functools.partial(apply, float(total) ** -0.5),
        out_shape=(
            jax.ShapeDtypeStruct((nblk, BLOCK, width), BF),
            jax.ShapeDtypeStruct((nblk, BLOCK), F32),
            jax.ShapeDtypeStruct((10, 128), F32),
        ),
        in_specs=[hbm] * 6,
        out_specs=(hbm, vmem, vmem),
        scratch_shapes=[
            pltpu.SMEM((1, BLOCK), jnp.int32),
            pltpu.VMEM((nblk, BLOCK, width), BF),
            pltpu.VMEM((nblk, BLOCK), F32),
            pltpu.VMEM((2, NR, listed_rows, 128), BF),
            pltpu.VMEM((NR, 8, BLOCK), F32),
            pltpu.VMEM((16, 128), F32),
            pltpu.VMEM((nblk, BLOCK, width), BF),
            pltpu.VMEM((nblk, BLOCK, width), F32),
            pltpu.VMEM((nblk, BLOCK), F32),
            dma((4,)),
            dma((9,)),
        ],
        compiler_params=pltpu.CompilerParams(vmem_limit_bytes=60 << 20),
        name="apply",
    )(blocks, table.reshape(nblk, BLOCK, width), state, rows, stats, dense)
    return (new_table.reshape(table.shape), new_accum.reshape(accum.shape), out.reshape(1280))


def solution(mesh):
    return jax.shard_map(
        on_device,
        mesh=mesh,
        in_specs=(
            P(("rep", "shard"), None, None),
            P("rep", "shard", None),
            P("shard", None),
            P("shard"),
            P("rep", "shard"),
            P("rep", "shard"),
            P(("rep", "shard"), None),
            P(),
            P(),
            P(),
            P(),
            P(("rep", "shard"), None),
        ),
        out_specs=(P("shard", None), P("shard"), P(("rep", "shard"))),
        check_vma=False,
    )
```
